32 devices in a mesh: groups: 2 (over y), dom: 8 (over z, x), event: 2 (over core).
Axes of the slice: x: 2, y: 2, z: 4, core: 2. Of those that a mesh axis runs over, the one named last changes fastest.
Arguments:
- wavefields: float32 [8, 12, 65536], P(('groups', 'event'), None, 'dom'), parts along dimension 0, may hold values from -6 to 6
- element_nodes: int32 [125, 1024], P(None, 'dom'), may hold values from 0 to 8191, as said below
- inverse_jacobian: float32 [9, 1024], P(None, 'dom'), may hold values from -0.45 to 1.6
- jacobian_det: float32 [1024], P('dom'), may hold values from 0.5 to 2
- moduli: float32 [2, 125, 1024], P(None, None, 'dom'), may hold values from 0.3 to 3
- inverse_mass: float32 [65536], P('dom'), may hold values from 0.02 to 0.06
- neighbours: int32 [8, 6], replicated, may hold values from 0 to 7, as said below
- shared_counts: int32 [8, 6], P('dom'), may hold values from 1 to 192, as said below
- shared_points: int32 [8, 6, 192], P('dom'), may hold values from 0 to 1023, as said below
Outputs:
- next_wavefields: float32 [8, 12, 65536], P(('groups', 'event'), None, 'dom'), parts along dimension 0
- sensitivity: float32 [4, 125, 1024], P('groups', None, ('dom', 'event')), parts along dimension 0
The draws below stay inside these ranges and needn't reach their ends.
There are 2 independent parts, one for each index of `groups`. The reference program is written for one: setup_inputs(seed, part) draws one part's arguments, and reference() takes and returns one part's arrays. A program takes and returns all parts, laid end to end along the dimension named above; an argument that names none is the same for every part. Nothing has to cross between parts.
Inputs may be any that keep to these rules, and one draw needn't show every extreme that they name: `neighbours`: each row lists 6 distinct partitions other than its own; if p lists d then d lists p. `shared_counts`: the count of d's slot naming p equals that of p's slot naming d; one count equals 192 in every draw. `shared_points`: entries at or past the slot's count are unused. `element_nodes`: elements 32 and later of each partition touch only points 1024 and above.
All inputs are finite; a program needn't handle non-finite values.
Results may differ from the reference program's by a relative error of at most 0.0001.
Values sent between devices are 32-bit elements; how exact they have to be, the bound alone decides.
A program may use at most 64 MiB of HBM per device.

```python
import math
import jax
import jax.numpy as jnp
import numpy as np
from jax import lax

NGLL = 5
ELEM = 128
NB = 6
CAP = 192
STEPS = 2
NLOC = 8192
BPTS = 1024
EB = 32
TOTAL_ELEM = 1024
TOTAL_PTS = 65536
EVENTS = 4
N_DOM = 8


def neighbour_graph(key):
    key_order, key_offset, key_size = jax.random.split(key, 3)
    ordering = jax.random.permutation(key_order, N_DOM)
    inverse = jnp.argsort(ordering)
    offsets = jax.random.permutation(key_offset, (N_DOM - 1) // 2)[:NB // 2] + 1
    slot_sizes = jax.random.randint(key_size, (NB // 2, N_DOM), 1, CAP + 1)
    slot_sizes = slot_sizes.at[0, 0].set(CAP).at[0, 1].set(1)
    forward = (ordering[:, None] + offsets[None, :]) % N_DOM
    backward = (ordering[:, None] - offsets[None, :]) % N_DOM
    halves = jnp.arange(NB // 2)[None, :]
    peer_ids = jnp.stack([inverse[forward], inverse[backward]], axis=2).reshape(N_DOM, NB)
    sizes_out = jnp.stack([slot_sizes[halves, ordering[:, None]], slot_sizes[halves, backward]], axis=2).reshape(N_DOM, NB)
    return (peer_ids.astype(jnp.int32), sizes_out.astype(jnp.int32))


def draw_neighbours(key, part):
    graph = neighbour_graph(key)
    return graph[0]


def draw_shared_counts(key, part):
    graph = neighbour_graph(key)
    return graph[1]


def draw_shared_points(key, part):
    key = jax.random.fold_in(key, 7)
    listed = jax.random.randint(key, (N_DOM, NB, CAP), 0, BPTS)
    listed = listed.at[0, 0, 0].set(BPTS - 1).at[0, 0, 1].set(0)
    return listed.astype(jnp.int32)


def draw_element_nodes(key, part):
    key = jax.random.fold_in(key, 11)
    key_outer, key_inner = jax.random.split(key)
    outer = jax.random.randint(key_outer, (NGLL ** 3, N_DOM, ELEM), 0, NLOC)
    inner = jax.random.randint(key_inner, (NGLL ** 3, N_DOM, ELEM), BPTS, NLOC)
    column = jnp.arange(ELEM)[None, None, :]
    chosen = jnp.where(column < EB, outer, inner)
    chosen = chosen.at[0, :, 0].set(0).at[0, :, ELEM - 1].set(NLOC - 1)
    return chosen.reshape(NGLL ** 3, N_DOM * ELEM).astype(jnp.int32)


def draw_inverse_jacobian(key, part):
    key = jax.random.fold_in(key, 17)
    key_diag, key_off = jax.random.split(key)
    diagonal = jax.random.uniform(key_diag, (9, TOTAL_ELEM), jnp.float32, 0.8, 1.6)
    offdiag = jnp.clip(0.2 * jax.random.normal(key_off, (9, TOTAL_ELEM), jnp.float32), -0.45, 0.45)
    on_diagonal = (jnp.arange(9) % 4 == 0)[:, None]
    return jnp.where(on_diagonal, diagonal, offdiag)


def block_levels(rng, shape, cuts, low, high):
    loudness = 1.0
    for position, blocks in cuts:
        draws = jax.random.uniform(jax.random.fold_in(jax.random.fold_in(rng, 6), position), (blocks,), jnp.float32, low / len(cuts), high / len(cuts))
        loudness = loudness * jnp.repeat(jnp.exp(draws), shape[position] // blocks).reshape((-1,) + (1,) * (len(shape) - 1 - position))
    return loudness


def normal_values(key, shape, deviation, reach, cuts=(), kind=jnp.bfloat16):
    values = deviation * jax.random.normal(key, shape, jnp.float32)
    if cuts:
        values = values * block_levels(key, shape, cuts, -0.22, 0.18)
    return jnp.clip(values, -reach, reach).astype(kind)


def setup_inputs(seed: int = 0, part: int = 0) -> dict:
    key_list = jax.random.split(jax.random.key(seed), 10)
    part_keys = jax.random.split(jax.random.fold_in(key_list[9], part), 10)
    return {
        "wavefields": normal_values(part_keys[0], (EVENTS, 12, TOTAL_PTS), 1.0, 6.0, ((0, 2), (2, 8)), jnp.float32),
        "element_nodes": draw_element_nodes(jax.random.fold_in(key_list[9], 71), part),
        "inverse_jacobian": draw_inverse_jacobian(jax.random.fold_in(key_list[9], 71), part),
        "jacobian_det": jnp.clip(jnp.exp(math.log(2.0) - 1.3862944 * jax.random.uniform(key_list[3], (TOTAL_ELEM,), jnp.float32) ** block_levels(key_list[3], (TOTAL_ELEM,), ((0, 8),), -0.2, 0.2)), 0.5, 2.0),
        "moduli": jnp.clip(jnp.exp(math.log(3.0) - 2.3025851 * jax.random.uniform(key_list[4], (2, NGLL ** 3, TOTAL_ELEM), jnp.float32) ** block_levels(key_list[4], (2, NGLL ** 3, TOTAL_ELEM), ((2, 8),), -0.2, 0.2)), 0.3, 3.0),
        "inverse_mass": jnp.clip(jnp.exp(math.log(0.06) - 1.0986123 * jax.random.uniform(key_list[5], (TOTAL_PTS,), jnp.float32) ** block_levels(key_list[5], (TOTAL_PTS,), ((0, 8),), -0.2, 0.2)), 0.02, 0.06),
        "neighbours": draw_neighbours(jax.random.fold_in(key_list[9], 71), part),
        "shared_counts": draw_shared_counts(jax.random.fold_in(key_list[9], 71), part),
        "shared_points": draw_shared_points(jax.random.fold_in(key_list[9], 71), part),
    }


time_step = 0.5
kernel_weight = 0.01
highest = lax.Precision.HIGHEST

def node_tables():
    points = np.array([-1.0, -np.sqrt(3.0 / 7.0), 0.0, np.sqrt(3.0 / 7.0), 1.0])
    legendre = (35.0 * points ** 4 - 30.0 * points ** 2 + 3.0) / 8.0
    derivative = np.zeros((5, 5))
    for a in range(5):
        for b in range(5):
            if a != b:
                derivative[a, b] = legendre[a] / (legendre[b] * (points[a] - points[b]))
    derivative[0, 0] = -5.0
    derivative[4, 4] = 5.0
    weights = np.array([0.1, 49.0 / 90.0, 32.0 / 45.0, 49.0 / 90.0, 0.1])
    cube_weights = weights[:, None, None] * weights[None, :, None] * weights[None, None, :]
    return (derivative, cube_weights)

def element_terms(displace, node_ids, inverse_jacobian, jacobian_det, moduli):
    derivative_np, cube_np = node_tables()
    derivative = jnp.asarray(derivative_np, jnp.float32)
    row_count = displace.shape[0]
    field_count = row_count // 3
    element_count = node_ids.shape[1]
    nodal_disp = jnp.take(displace, node_ids, axis=1).reshape(field_count, 3, 5, 5, 5, element_count)
    along_ref = (jnp.einsum('ai,fckjie->fckjae', derivative, nodal_disp, precision=highest), jnp.einsum('aj,fckjie->fckaie', derivative, nodal_disp, precision=highest), jnp.einsum('ak,fckjie->fcajie', derivative, nodal_disp, precision=highest))
    jacobian = inverse_jacobian.reshape(3, 3, element_count)
    gradient = [along_ref[0] * jacobian[0, m] + along_ref[1] * jacobian[1, m] + along_ref[2] * jacobian[2, m] for m in range(3)]
    divergence = gradient[0][:, 0] + gradient[1][:, 1] + gradient[2][:, 2]
    blocks = moduli.reshape(2, 5, 5, 5, element_count)
    shear_mod = blocks[0]
    bulk_mod = blocks[1]
    lame_first = bulk_mod - 2.0 / 3.0 * shear_mod
    volume = jnp.asarray(cube_np, jnp.float32)[:, :, :, None] * jacobian_det
    forces = []
    deviator_sum = jnp.zeros((5, 5, 5, element_count), jnp.float32)
    for c in range(3):
        stress = []
        for m in range(3):
            strain = 0.5 * (gradient[m][:, c] + gradient[c][:, m])
            component = 2.0 * shear_mod * strain
            if m == c:
                component = component + lame_first * divergence
                deviator = strain - divergence / 3.0
            else:
                deviator = strain
            stress.append(component)
            paired = deviator.reshape(field_count // 2, 2, 5, 5, 5, element_count)
            deviator_sum = deviator_sum + lax.optimization_barrier(jnp.sum(paired[:, 0] * paired[:, 1], axis=0))
        traction = [volume * (stress[0] * jacobian[d, 0] + stress[1] * jacobian[d, 1] + stress[2] * jacobian[d, 2]) for d in range(3)]
        component_force = jnp.einsum('ia,fkjie->fkjae', derivative, traction[0], precision=highest)
        component_force = component_force + jnp.einsum('ja,fkjie->fkaie', derivative, traction[1], precision=highest)
        component_force = component_force + jnp.einsum('ka,fkjie->fajie', derivative, traction[2], precision=highest)
        forces.append(component_force)
    element_force = jnp.stack(forces, axis=1).reshape(row_count, -1)
    paired_div = divergence.reshape(field_count // 2, 2, 5, 5, 5, element_count)
    bulk_term = bulk_mod * lax.optimization_barrier(jnp.sum(paired_div[:, 0] * paired_div[:, 1], axis=0))
    shear_term = 2.0 * shear_mod * deviator_sum
    kernel_terms = jnp.stack([shear_term, bulk_term]).reshape(2, 125, element_count)
    return (element_force, kernel_terms)

def assemble(element_force, node_ids, point_count):
    empty = jnp.zeros((element_force.shape[0], point_count), jnp.float32)
    return empty.at[:, node_ids.reshape(-1)].add(element_force)

def reference(wavefields, element_nodes, inverse_jacobian, jacobian_det, moduli, inverse_mass, neighbours, shared_counts, shared_points):
    events = wavefields.shape[0]
    row_count = events * 6
    parted = wavefields.reshape(events, 2, 2, 3, N_DOM, NLOC)
    present = parted[:, :, 0].reshape(row_count, N_DOM, NLOC).transpose(1, 0, 2)
    earlier = parted[:, :, 1].reshape(row_count, N_DOM, NLOC).transpose(1, 0, 2)
    nodes_part = element_nodes.reshape(NGLL ** 3, N_DOM, ELEM).transpose(1, 0, 2)
    jacobian_part = inverse_jacobian.reshape(9, N_DOM, ELEM).transpose(1, 0, 2)
    determinant_part = jacobian_det.reshape(N_DOM, ELEM)
    modulus_part = moduli.reshape(2, NGLL ** 3, N_DOM, ELEM).transpose(2, 0, 1, 3)
    mass_part = inverse_mass.reshape(N_DOM, NLOC)
    domain_ids = jnp.arange(N_DOM, dtype=jnp.int32)
    back_slot = jnp.argmax(neighbours[neighbours] == domain_ids[:, None, None], axis=2).astype(jnp.int32)
    source = shared_points[neighbours, back_slot]
    slot_live = (jnp.arange(CAP, dtype=jnp.int32)[None, None, :] < shared_counts[:, :, None]).astype(jnp.float32)
    totals = jnp.zeros((N_DOM, 2, NGLL ** 3, ELEM), jnp.float32)
    for step_index in range(STEPS):

        def local_part(pieces):
            present_rows, node_ids, jacobian, determinant, modulus = pieces
            element_force, kernel_terms = element_terms(present_rows, node_ids, jacobian, determinant, modulus)
            return (assemble(element_force, node_ids, NLOC), kernel_terms)
        local_force, kernel_terms = lax.map(local_part, (present, nodes_part, jacobian_part, determinant_part, modulus_part))
        totals = totals + kernel_terms

        def with_halo(domain):
            peer_force = jnp.take(local_force, neighbours[domain], axis=0)
            picked = jnp.take_along_axis(peer_force, source[domain][:, None, :], axis=2) * slot_live[domain][:, None, :]
            flat = picked.transpose(1, 0, 2).reshape(row_count, -1)
            return local_force[domain].at[:, shared_points[domain].reshape(-1)].add(flat)
        assembled = lax.map(with_halo, domain_ids)
        following = 2.0 * present - earlier - time_step * time_step * mass_part[:, None, :] * assembled
        earlier = present
        present = following
    sensitivity = (kernel_weight * time_step * totals).transpose(1, 2, 0, 3).reshape(2, NGLL ** 3, N_DOM * ELEM)

    def unpart(stacked):
        return stacked.transpose(1, 0, 2).reshape(events, 2, 3, N_DOM * NLOC)
    next_wavefields = jnp.stack([unpart(present), unpart(earlier)], axis=2).reshape(events, 12, N_DOM * NLOC)
    return (next_wavefields, sensitivity)
```

```python
import jax
import jax.numpy as jnp
import numpy as np
from jax import lax
from jax.experimental import pallas as pl
from jax.experimental.pallas import tpu as pltpu
from jax.sharding import PartitionSpec as P

STEPS = 2
WIDE = 256
NOWHERE = 1 << 24

time_step = 0.5
kernel_weight = 0.01
highest = lax.Precision.HIGHEST
f32 = jnp.float32
bf16 = jnp.bfloat16


def node_tables():
    points = np.array([-1.0, -np.sqrt(3.0 / 7.0), 0.0, np.sqrt(3.0 / 7.0), 1.0])
    legendre = (35.0 * points**4 - 30.0 * points**2 + 3.0) / 8.0
    derivative = np.zeros((5, 5))
    for a in range(5):
        for b in range(5):
            if a != b:
                derivative[a, b] = legendre[a] / (legendre[b] * (points[a] - points[b]))
    derivative[0, 0] = -5.0
    derivative[4, 4] = 5.0
    weights = np.array([0.1, 49.0 / 90.0, 32.0 / 45.0, 49.0 / 90.0, 0.1])
    cube_weights = weights[:, None, None] * weights[None, :, None] * weights[None, None, :]
    return (derivative, cube_weights)


def padded_tables():
    derivative, cube = node_tables()
    eye = np.eye(5)
    along = (
        np.kron(eye, np.kron(eye, derivative)),
        np.kron(eye, np.kron(derivative, eye)),
        np.kron(derivative, np.kron(eye, eye)),
    )
    forward = np.zeros((3 * 128, 128), np.float32)
    backward = np.zeros((128, 3 * 128), np.float32)
    for d in range(3):
        forward[d * 128 : d * 128 + 125, :125] = along[d]
        backward[:125, d * 128 : d * 128 + 125] = along[d].T
    volume = np.zeros((128, 128), np.float32)
    volume[:125] = cube.reshape(125, 1)
    return forward, backward, volume


def split(values):
    upper = values.astype(bf16)
    lower = (values - upper.astype(f32)).astype(bf16)
    return upper, lower


def columns_onehot(column_ids):
    rows = lax.broadcasted_iota(jnp.int32, (WIDE, column_ids.shape[1]), 0)
    return jnp.where(rows == column_ids, 1.0, 0.0).astype(bf16)


def pick_rows(result, row_ids, group):
    mask = lax.broadcasted_iota(jnp.int32, (group, 128), 0) == row_ids
    return [
        jnp.sum(
            jnp.where(mask, result[c * group : (c + 1) * group], 0.0), axis=0, keepdims=True
        )
        for c in range(12)
    ]


def slot_onehot(slots_ref):
    return jnp.concatenate(
        [columns_onehot(slots_ref[r : r + 1, :] & (WIDE - 1)) for r in range(12)], axis=1
    )


def combine(present_ref, earlier_ref, force_ref, arrived_ref, mass_ref, slots_ref, peers_ref, following_ref):
    domains = arrived_ref.shape[0]
    rows = mass_ref.shape[0]
    blocks = []
    for k in range(6):
        block = jnp.zeros((12, WIDE), f32)
        for p in range(domains):
            block = jnp.where(peers_ref[0, k] == p, arrived_ref[p], block)
        blocks.append(block)
    received = jnp.concatenate(blocks, axis=1)
    onehot = slot_onehot(slots_ref)
    pieces = []
    for r in range(12):
        mask = lax.broadcasted_iota(jnp.int32, (8, 128), 0) == (slots_ref[r : r + 1, :] >> 8)
        part = received[:, r * 128 : (r + 1) * 128]
        pieces.append(
            jnp.concatenate(
                [jnp.where(mask, part[c : c + 1, :], 0.0) for c in range(12)], axis=0
            )
        )
    spread = jnp.concatenate(pieces, axis=1)
    upper, lower = split(spread)
    both = lax.dot_general(
        jnp.concatenate([upper, lower], axis=0), onehot, (((1,), (1,)), ((), ())),
        preferred_element_type=f32,
    )
    added = both[:96] + both[96:]
    mass = mass_ref[...] * (time_step * time_step)
    for c in range(12):
        where = slice(c * rows, (c + 1) * rows)
        force = force_ref[where, :]
        total = jnp.concatenate([force[:8] + added[c * 8 : (c + 1) * 8], force[8:]], axis=0)
        following_ref[where, :] = 2.0 * present_ref[where, :] - earlier_ref[where, :] - mass * total


def forces(
    present_ref, ids_ref, jacobian_ref, det_ref, moduli_ref, slots_ref, peers_ref,
    forward_ref, backward_ref, volume_ref,
    force_ref, sending_ref, terms_ref,
    onehot_ref, nodal_ref, along_ref, traction_ref, nodal_force_ref, sum_ref,
):
    rows = present_ref.shape[0] // 12
    upper, lower = split(present_ref[...])
    table = jnp.concatenate([upper, lower], axis=1)
    sublane = lax.broadcasted_iota(jnp.int32, (8, 128), 0)

    def gather(g, carry):
        base = pl.multiple_of(g * 8, 8)
        ids = ids_ref[pl.ds(base, 8), :]
        onehot = jnp.concatenate(
            [columns_onehot((ids & (WIDE - 1))[r : r + 1, :]) for r in range(8)], axis=1
        )
        onehot_ref[g] = onehot
        result = jnp.dot(
            table, jnp.concatenate([onehot, onehot], axis=0), preferred_element_type=f32
        )
        row_ids = ids >> 8
        gathered = [jnp.zeros((8, 128), f32)] * 12
        for r in range(8):
            picked = pick_rows(result[:, r * 128 : (r + 1) * 128], row_ids[r : r + 1, :], rows)
            gathered = [jnp.where(sublane == r, picked[c], gathered[c]) for c in range(12)]
        nodal_ref[pl.ds(base, 8), :] = jnp.concatenate(gathered, axis=1)
        return carry

    lax.fori_loop(0, 16, gather, 0)
    along_ref[...] = jnp.dot(
        forward_ref[...], nodal_ref[...], precision=highest, preferred_element_type=f32
    )

    def elements(g, carry):
        base = pl.multiple_of(g * 8, 8)
        jac = [jnp.broadcast_to(jacobian_ref[i : i + 1, :], (8, 128)) for i in range(9)]
        shear = moduli_ref[0, pl.ds(base, 8), :]
        bulk = moduli_ref[1, pl.ds(base, 8), :]
        lame = bulk - 2.0 / 3.0 * shear
        volume = volume_ref[pl.ds(base, 8), :] * det_ref[...]
        scaled = [volume * jac[i] for i in range(9)]
        shear_sum = jnp.zeros((8, 128), f32)
        bulk_sum = jnp.zeros((8, 128), f32)
        for event in range(2):
            kept = []
            for field in range(2):
                first = (event * 2 + field) * 3
                local = [
                    [
                        along_ref[pl.ds(d * 128 + base, 8), (first + c) * 128 : (first + c + 1) * 128]
                        for c in range(3)
                    ]
                    for d in range(3)
                ]
                grad = [
                    [
                        local[0][c] * jac[m] + local[1][c] * jac[3 + m] + local[2][c] * jac[6 + m]
                        for c in range(3)
                    ]
                    for m in range(3)
                ]
                div = grad[0][0] + grad[1][1] + grad[2][2]
                strain = {}
                stress = {}
                deviator = {}
                for c in range(3):
                    for m in range(c, 3):
                        if c == m:
                            strain[c, m] = grad[c][c]
                            deviator[c, m] = strain[c, m] - div * (1.0 / 3.0)
                            stress[c, m] = 2.0 * shear * strain[c, m] + lame * div
                        else:
                            twice = grad[m][c] + grad[c][m]
                            strain[c, m] = 0.5 * twice
                            deviator[c, m] = strain[c, m]
                            stress[c, m] = shear * twice
                            stress[m, c] = stress[c, m]
                kept.append((deviator, div))
                for c in range(3):
                    for d in range(3):
                        traction_ref[
                            pl.ds(d * 128 + base, 8), (first + c) * 128 : (first + c + 1) * 128
                        ] = (
                            stress[c, 0] * scaled[3 * d]
                            + stress[c, 1] * scaled[3 * d + 1]
                            + stress[c, 2] * scaled[3 * d + 2]
                        )
            (dev0, div0), (dev1, div1) = kept
            bulk_sum = bulk_sum + div0 * div1
            for c in range(3):
                for m in range(c, 3):
                    product = dev0[c, m] * dev1[c, m]
                    shear_sum = shear_sum + (product if c == m else 2.0 * product)
        terms_ref[0, pl.ds(base, 8), :] += 2.0 * shear * shear_sum
        terms_ref[1, pl.ds(base, 8), :] += bulk * bulk_sum
        return carry

    lax.fori_loop(0, 16, elements, 0)
    nodal_force_ref[...] = jnp.dot(
        backward_ref[...], traction_ref[...], precision=highest, preferred_element_type=f32
    )
    sum_ref[...] = jnp.zeros_like(sum_ref)

    def scatter(g, carry):
        base = pl.multiple_of(g * 8, 8)
        row_ids = ids_ref[pl.ds(base, 8), :] >> 8
        values = nodal_force_ref[pl.ds(base, 8), :]
        high = values.astype(bf16).astype(f32)
        low = values - high
        pieces = []
        for r in range(8):
            mask = lax.broadcasted_iota(jnp.int32, (rows, 128), 0) == row_ids[r : r + 1, :]
            pieces.append(
                jnp.concatenate(
                    [
                        jnp.where(mask, part[r : r + 1, c * 128 : (c + 1) * 128], 0.0).astype(bf16)
                        for part in (high, low)
                        for c in range(12)
                    ],
                    axis=0,
                )
            )
        sum_ref[...] += lax.dot_general(
            jnp.concatenate(pieces, axis=1), onehot_ref[g], (((1,), (1,)), ((), ())),
            preferred_element_type=f32,
        )
        return carry

    lax.fori_loop(0, 16, scatter, 0)
    half = sum_ref.shape[0] // 2
    force_ref[...] = sum_ref[:half, :] + sum_ref[half:, :]

    border = jnp.concatenate([force_ref[c * rows : c * rows + 8, :] for c in range(12)], axis=0)
    upper, lower = split(border)
    onehot = slot_onehot(slots_ref)
    result = jnp.dot(
        jnp.concatenate([upper, lower], axis=1),
        jnp.concatenate([onehot, onehot], axis=0),
        preferred_element_type=f32,
    )
    outgoing = []
    for r in range(12):
        picked = pick_rows(result[:, r * 128 : (r + 1) * 128], slots_ref[r : r + 1, :] >> 8, 8)
        outgoing.append(jnp.concatenate(picked, axis=0))
    for p in range(sending_ref.shape[0]):
        block = jnp.zeros((12, WIDE), f32)
        for k in range(6):
            block = jnp.where(
                peers_ref[0, k] == p,
                jnp.concatenate([outgoing[2 * k], outgoing[2 * k + 1]], axis=1),
                block,
            )
        sending_ref[p] = block


def first_step(present_ref, *refs):
    refs[11][...] = jnp.zeros_like(refs[11])
    forces(present_ref, *refs)


def next_step(
    present_ref, earlier_ref, old_force_ref, arrived_ref, mass_ref, old_terms_ref,
    ids_ref, jacobian_ref, det_ref, moduli_ref, slots_ref, peers_ref,
    forward_ref, backward_ref, volume_ref,
    following_ref, force_ref, sending_ref, terms_ref, *scratch
):
    combine(present_ref, earlier_ref, old_force_ref, arrived_ref, mass_ref, slots_ref, peers_ref, following_ref)
    terms_ref[...] = old_terms_ref[...]
    forces(
        following_ref, ids_ref, jacobian_ref, det_ref, moduli_ref, slots_ref, peers_ref,
        forward_ref, backward_ref, volume_ref, force_ref, sending_ref, terms_ref, *scratch
    )


def per_device(
    wavefields,
    element_nodes,
    inverse_jacobian,
    jacobian_det,
    moduli,
    inverse_mass,
    neighbours,
    shared_counts,
    shared_points,
):
    events, _, point_count = wavefields.shape
    rows = point_count // WIDE
    domains = neighbours.shape[0]
    element_count = element_nodes.shape[1]
    parted = wavefields.reshape(events, 2, 2, 3 * rows, WIDE)
    present = parted[:, :, 0].reshape(12 * rows, WIDE)
    earlier = parted[:, :, 1].reshape(12 * rows, WIDE)
    mass = inverse_mass.reshape(rows, WIDE)
    ids = jnp.pad(element_nodes, ((0, 3), (0, 0)), constant_values=NOWHERE)
    own = lax.axis_index("dom")
    peers = lax.dynamic_slice_in_dim(neighbours, own, 1, 0)
    slot_count, capacity = shared_points.shape[1:]
    live = jnp.arange(capacity, dtype=jnp.int32)[None, :] < shared_counts[0][:, None]
    slots = jnp.where(live, shared_points[0], NOWHERE)
    slots = jnp.pad(slots, ((0, 0), (0, WIDE - capacity)), constant_values=NOWHERE)
    slots = slots.reshape(12, 128)
    moduli = jnp.pad(moduli, ((0, 0), (0, 3), (0, 0)))
    det = jacobian_det.reshape(1, element_count)
    forward, backward, volume = (jnp.asarray(table) for table in padded_tables())
    common = (ids, inverse_jacobian, det, moduli, slots, peers, forward, backward, volume)
    vmem = pl.BlockSpec(memory_space=pltpu.VMEM)
    smem = pl.BlockSpec(memory_space=pltpu.SMEM)
    common_specs = [vmem, vmem, vmem, vmem, vmem, smem, vmem, vmem, vmem]
    state = jax.ShapeDtypeStruct((12 * rows, WIDE), f32)
    made = (
        state,
        jax.ShapeDtypeStruct((domains, 12, WIDE), f32),
        jax.ShapeDtypeStruct((2, 128, 128), f32),
    )
    scratch = [
        pltpu.VMEM((16, WIDE, 1024), bf16),
        pltpu.VMEM((128, 12 * 128), f32),
        pltpu.VMEM((3 * 128, 12 * 128), f32),
        pltpu.VMEM((3 * 128, 12 * 128), f32),
        pltpu.VMEM((128, 12 * 128), f32),
        pltpu.VMEM((24 * rows, WIDE), f32),
    ]
    params = pltpu.CompilerParams(vmem_limit_bytes=50 * 1024 * 1024)

    def exchange(sending):
        return lax.all_to_all(sending, "dom", split_axis=0, concat_axis=0, tiled=True)

    force, sending, terms = pl.pallas_call(
        first_step,
        out_shape=made,
        in_specs=[vmem] + common_specs,
        out_specs=(vmem,) * 3,
        scratch_shapes=scratch,
        compiler_params=params,
    )(present, *common)
    for _ in range(STEPS - 1):
        arrived = exchange(sending)
        following, force, sending, terms = pl.pallas_call(
            next_step,
            out_shape=(state,) + made,
            in_specs=[vmem] * 6 + common_specs,
            out_specs=(vmem,) * 4,
            scratch_shapes=scratch,
            compiler_params=params,
        )(present, earlier, force, arrived, mass, terms, *common)
        earlier, present = present, following
    arrived = exchange(sending)
    following = pl.pallas_call(
        combine,
        out_shape=state,
        in_specs=[vmem] * 6 + [smem],
        out_specs=vmem,
        compiler_params=params,
    )(present, earlier, force, arrived, mass, slots, peers)
    earlier, present = present, following

    sharers = lax.axis_size("event")
    share_width = element_count // sharers
    spot = lax.axis_index("event")
    terms = terms[:, :125]
    if sharers == 2:
        low, high = terms[:, :, :share_width], terms[:, :, share_width:]
        theirs = lax.ppermute(jnp.where(spot == 0, high, low), "event", [(0, 1), (1, 0)])
        summed = jnp.where(spot == 0, low, high) + theirs
    else:
        summed = lax.dynamic_slice_in_dim(
            lax.psum(terms, "event"), spot * share_width, share_width, 2
        )
    sensitivity = kernel_weight * time_step * summed
    next_wavefields = jnp.stack(
        [present.reshape(events, 2, 3, point_count), earlier.reshape(events, 2, 3, point_count)],
        axis=2,
    ).reshape(events, 12, point_count)
    return (next_wavefields, sensitivity)


def solution(mesh):
    return jax.shard_map(
        per_device,
        mesh=mesh,
        in_specs=(
            P(("groups", "event"), None, "dom"),
            P(None, "dom"),
            P(None, "dom"),
            P("dom"),
            P(None, None, "dom"),
            P("dom"),
            P(),
            P("dom", None),
            P("dom", None, None),
        ),
        out_specs=(P(("groups", "event"), None, "dom"), P("groups", None, ("dom", "event"))),
        check_vma=False,
    )
```

```python
import jax
import jax.numpy as jnp
import numpy as np
from jax import lax
from jax.experimental import pallas as pl
from jax.experimental.pallas import tpu as pltpu
from jax.sharding import PartitionSpec as P

STEPS = 2
WIDE = 256
NOWHERE = 1 << 24

time_step = 0.5
kernel_weight = 0.01
highest = lax.Precision.HIGHEST
f32 = jnp.float32
bf16 = jnp.bfloat16


def node_tables():
    points = np.array([-1.0, -np.sqrt(3.0 / 7.0), 0.0, np.sqrt(3.0 / 7.0), 1.0])
    legendre = (35.0 * points**4 - 30.0 * points**2 + 3.0) / 8.0
    derivative = np.zeros((5, 5))
    for a in range(5):
        for b in range(5):
            if a != b:
                derivative[a, b] = legendre[a] / (legendre[b] * (points[a] - points[b]))
    derivative[0, 0] = -5.0
    derivative[4, 4] = 5.0
    weights = np.array([0.1, 49.0 / 90.0, 32.0 / 45.0, 49.0 / 90.0, 0.1])
    cube_weights = weights[:, None, None] * weights[None, :, None] * weights[None, None, :]
    return (derivative, cube_weights)


def padded_tables():
    derivative, cube = node_tables()
    eye = np.eye(5)
    along = (
        np.kron(eye, np.kron(eye, derivative)),
        np.kron(eye, np.kron(derivative, eye)),
        np.kron(derivative, np.kron(eye, eye)),
    )
    forward = np.zeros((3 * 128, 128), np.float32)
    backward = np.zeros((128, 3 * 128), np.float32)
    for d in range(3):
        forward[d * 128 : d * 128 + 125, :125] = along[d]
        backward[:125, d * 128 : d * 128 + 125] = along[d].T
    volume = np.zeros((128, 128), np.float32)
    volume[:125] = cube.reshape(125, 1)
    return forward, backward, volume


def split(values):
    upper = values.astype(bf16)
    lower = (values - upper.astype(f32)).astype(bf16)
    return upper, lower


def columns_onehot(column_ids):
    return onehot_rows(column_ids, WIDE)


def onehot_rows(row_ids, count):
    rows = lax.broadcasted_iota(jnp.int32, (count, 128), 0).astype(f32).astype(bf16)
    wanted = jnp.broadcast_to(row_ids.astype(f32), (count, 128)).astype(bf16)
    return jnp.where(rows == wanted, jnp.ones((), bf16), jnp.zeros((), bf16))


def pick_rows(result, row_ids, group):
    mask = lax.broadcasted_iota(jnp.int32, (group, 128), 0) == row_ids
    return [
        jnp.sum(
            jnp.where(mask, result[c * group : (c + 1) * group], 0.0), axis=0, keepdims=True
        )
        for c in range(12)
    ]


def sum_sublanes(parts, sublane):
    for width in (4, 2, 1):
        first = (sublane & width) == 0
        merged = []
        for r in range(width):
            near = jnp.where(first, parts[r], parts[r + width])
            far = jnp.where(first, parts[r + width], parts[r])
            if width == 4:
                far = pltpu.roll(far, 4, 0)
            else:
                far = jnp.where(first, pltpu.roll(far, 8 - width, 0), pltpu.roll(far, width, 0))
            merged.append(near + far)
        parts = merged
    return parts[0]


def split_product(left, right):
    left_upper, left_lower = split(left)
    right_upper, right_lower = split(right)
    return jnp.dot(
        jnp.concatenate([left_upper, left_lower, left_upper], axis=1),
        jnp.concatenate([right_upper, right_upper, right_lower], axis=0),
        preferred_element_type=f32,
    )


def slot_onehot(slots_ref):
    return jnp.concatenate(
        [columns_onehot(slots_ref[r : r + 1, :] & (WIDE - 1)) for r in range(12)], axis=1
    )


def combine(present_ref, earlier_ref, force_ref, arrived_ref, mass_ref, slots_ref, peers_ref, following_ref):
    domains = arrived_ref.shape[0]
    rows = mass_ref.shape[0]
    blocks = []
    for k in range(6):
        block = jnp.zeros((16, WIDE), f32)
        for p in range(domains):
            block = jnp.where(peers_ref[0, k] == p, arrived_ref[p], block)
        blocks.append(block)
    received = jnp.concatenate(blocks, axis=1)
    onehot = slot_onehot(slots_ref)
    pieces = []
    for r in range(12):
        mask = lax.broadcasted_iota(jnp.int32, (8, 128), 0) == (slots_ref[r : r + 1, :] >> 8)
        part = received[:, r * 128 : (r + 1) * 128]
        pieces.append(
            jnp.concatenate(
                [jnp.where(mask, part[c : c + 1, :], 0.0) for c in range(12)], axis=0
            )
        )
    spread = jnp.concatenate(pieces, axis=1)
    upper, lower = split(spread)
    both = lax.dot_general(
        jnp.concatenate([upper, lower], axis=0), onehot, (((1,), (1,)), ((), ())),
        preferred_element_type=f32,
    )
    added = both[:96] + both[96:]
    mass = mass_ref[...] * (time_step * time_step)
    for c in range(12):
        where = slice(c * rows, (c + 1) * rows)
        force = force_ref[where, :]
        total = jnp.concatenate([force[:8] + added[c * 8 : (c + 1) * 8], force[8:]], axis=0)
        following_ref[where, :] = 2.0 * present_ref[where, :] - earlier_ref[where, :] - mass * total


def forces(
    present_ref, ids_ref, jacobian_ref, det_ref, moduli_ref, slots_ref, peers_ref,
    forward_ref, backward_ref, volume_ref,
    force_ref, sending_ref, terms_ref,
    nodal_ref, along_ref, traction_ref, nodal_force_ref, sum_ref,
):
    rows = present_ref.shape[0] // 12
    sublane = lax.broadcasted_iota(jnp.int32, (8, 128), 0)
    tiles = rows // 8

    def gather(g, carry):
        base = pl.multiple_of(g * 8, 8)
        ids = ids_ref[pl.ds(base, 8), :]
        lanes = [jnp.broadcast_to((ids & 127)[r : r + 1, :], (8, 128)) for r in range(8)]
        keys = ids >> 7
        masks = []
        for r in range(8):
            key = jnp.broadcast_to(keys[r : r + 1, :], (8, 128)) - 2 * sublane
            masks.append([key == 16 * t + h for t in range(tiles) for h in range(2)])
        for c in range(12):
            found = [jnp.zeros((8, 128), f32)] * 8
            for t in range(tiles):
                for h in range(2):
                    tile = present_ref[c * rows + t * 8 : c * rows + t * 8 + 8, h * 128 : h * 128 + 128]
                    for r in range(8):
                        taken = jnp.take_along_axis(tile, lanes[r], axis=1, mode="promise_in_bounds")
                        found[r] = jnp.where(masks[r][2 * t + h], taken, found[r])
            nodal_ref[pl.ds(base, 8), c * 128 : (c + 1) * 128] = sum_sublanes(found, sublane)
        return carry

    lax.fori_loop(0, 16, gather, 0)
    along_ref[...] = split_product(forward_ref[...], nodal_ref[...])

    def elements(g, carry):
        base = pl.multiple_of(g * 8, 8)
        jac = [jnp.broadcast_to(jacobian_ref[i : i + 1, :], (8, 128)) for i in range(9)]
        shear = moduli_ref[0, pl.ds(base, 8), :]
        bulk = moduli_ref[1, pl.ds(base, 8), :]
        lame = bulk - 2.0 / 3.0 * shear
        volume = volume_ref[pl.ds(base, 8), :] * det_ref[...]
        scaled = [volume * jac[i] for i in range(9)]
        shear_sum = jnp.zeros((8, 128), f32)
        bulk_sum = jnp.zeros((8, 128), f32)
        for event in range(2):
            kept = []
            for field in range(2):
                first = (event * 2 + field) * 3
                local = [
                    [
                        along_ref[pl.ds(d * 128 + base, 8), (first + c) * 128 : (first + c + 1) * 128]
                        for c in range(3)
                    ]
                    for d in range(3)
                ]
                grad = [
                    [
                        local[0][c] * jac[m] + local[1][c] * jac[3 + m] + local[2][c] * jac[6 + m]
                        for c in range(3)
                    ]
                    for m in range(3)
                ]
                div = grad[0][0] + grad[1][1] + grad[2][2]
                strain = {}
                stress = {}
                deviator = {}
                for c in range(3):
                    for m in range(c, 3):
                        if c == m:
                            strain[c, m] = grad[c][c]
                            deviator[c, m] = strain[c, m] - div * (1.0 / 3.0)
                            stress[c, m] = 2.0 * shear * strain[c, m] + lame * div
                        else:
                            twice = grad[m][c] + grad[c][m]
                            strain[c, m] = 0.5 * twice
                            deviator[c, m] = strain[c, m]
                            stress[c, m] = shear * twice
                            stress[m, c] = stress[c, m]
                kept.append((deviator, div))
                for c in range(3):
                    for d in range(3):
                        traction_ref[
                            pl.ds(d * 128 + base, 8), (first + c) * 128 : (first + c + 1) * 128
                        ] = (
                            stress[c, 0] * scaled[3 * d]
                            + stress[c, 1] * scaled[3 * d + 1]
                            + stress[c, 2] * scaled[3 * d + 2]
                        )
            (dev0, div0), (dev1, div1) = kept
            bulk_sum = bulk_sum + div0 * div1
            for c in range(3):
                for m in range(c, 3):
                    product = dev0[c, m] * dev1[c, m]
                    shear_sum = shear_sum + (product if c == m else 2.0 * product)
        terms_ref[0, pl.ds(base, 8), :] += 2.0 * shear * shear_sum
        terms_ref[1, pl.ds(base, 8), :] += bulk * bulk_sum
        return carry

    lax.fori_loop(0, 16, elements, 0)
    nodal_force_ref[...] = split_product(backward_ref[...], traction_ref[...])
    sum_ref[...] = jnp.zeros_like(sum_ref)

    def scatter(g, carry):
        base = pl.multiple_of(g * 8, 8)
        row_ids = ids_ref[pl.ds(base, 8), :] >> 8
        values = nodal_force_ref[pl.ds(base, 8), :]
        high = values.astype(bf16).astype(f32)
        low = values - high
        pieces = []
        columns = []
        for r in range(8):
            columns.append(columns_onehot((ids_ref[pl.ds(base, 8), :] & (WIDE - 1))[r : r + 1, :]))
            chosen = onehot_rows(row_ids[r : r + 1, :], rows)
            blocks = []
            for part in (high, low):
                for c in range(12):
                    row = jnp.broadcast_to(part[r : r + 1, c * 128 : (c + 1) * 128], (16, 128))
                    row = row.astype(bf16)
                    blocks += [chosen[t : t + 16] * row for t in range(0, rows, 16)]
            pieces.append(jnp.concatenate(blocks, axis=0))
        sum_ref[...] += lax.dot_general(
            jnp.concatenate(pieces, axis=1), jnp.concatenate(columns, axis=1),
            (((1,), (1,)), ((), ())), preferred_element_type=f32,
        )
        return carry

    lax.fori_loop(0, 16, scatter, 0)
    half = sum_ref.shape[0] // 2
    force_ref[...] = sum_ref[:half, :] + sum_ref[half:, :]

    border = jnp.concatenate([force_ref[c * rows : c * rows + 8, :] for c in range(12)], axis=0)
    upper, lower = split(border)
    onehot = slot_onehot(slots_ref)
    result = jnp.dot(
        jnp.concatenate([upper, lower], axis=1),
        jnp.concatenate([onehot, onehot], axis=0),
        preferred_element_type=f32,
    )
    outgoing = []
    for r in range(12):
        picked = pick_rows(result[:, r * 128 : (r + 1) * 128], slots_ref[r : r + 1, :] >> 8, 8)
        outgoing.append(jnp.concatenate(picked + [jnp.zeros((4, 128), f32)], axis=0))
    for p in range(sending_ref.shape[0]):
        block = jnp.zeros((16, WIDE), f32)
        for k in range(6):
            block = jnp.where(
                peers_ref[0, k] == p,
                jnp.concatenate([outgoing[2 * k], outgoing[2 * k + 1]], axis=1),
                block,
            )
        sending_ref[p] = block


def swap_blocks(sending_ref, arrived_ref, send_sem, recv_sem):
    domains = sending_ref.shape[0]
    me = lax.axis_index("dom")
    barrier = pltpu.get_barrier_semaphore()
    for offset in range(1, domains):
        pl.semaphore_signal(
            barrier, inc=1, device_id={"dom": lax.rem(me + offset, domains)},
            device_id_type=pl.DeviceIdType.MESH,
        )
    pl.semaphore_wait(barrier, domains - 1)
    copies = []
    for offset in range(1, domains):
        target = lax.rem(me + offset, domains)
        copies.append(
            pltpu.make_async_remote_copy(
                src_ref=sending_ref.at[target],
                dst_ref=arrived_ref.at[me],
                send_sem=send_sem.at[offset],
                recv_sem=recv_sem.at[offset],
                device_id={"dom": target},
                device_id_type=pl.DeviceIdType.MESH,
            )
        )
        copies[-1].start()
    arrived_ref[me] = sending_ref[me]
    for copy in copies:
        copy.wait()


def first_step(present_ref, *refs):
    refs[11][...] = jnp.zeros_like(refs[11])
    forces(present_ref, *refs)


def next_step(
    present_ref, earlier_ref, old_force_ref, arrived_ref, mass_ref, old_terms_ref,
    ids_ref, jacobian_ref, det_ref, moduli_ref, slots_ref, peers_ref,
    forward_ref, backward_ref, volume_ref,
    following_ref, force_ref, sending_ref, terms_ref, *scratch
):
    combine(present_ref, earlier_ref, old_force_ref, arrived_ref, mass_ref, slots_ref, peers_ref, following_ref)
    terms_ref[...] = old_terms_ref[...]
    forces(
        following_ref, ids_ref, jacobian_ref, det_ref, moduli_ref, slots_ref, peers_ref,
        forward_ref, backward_ref, volume_ref, force_ref, sending_ref, terms_ref, *scratch
    )


def per_device(
    wavefields,
    element_nodes,
    inverse_jacobian,
    jacobian_det,
    moduli,
    inverse_mass,
    neighbours,
    shared_counts,
    shared_points,
):
    events, _, point_count = wavefields.shape
    rows = point_count // WIDE
    domains = neighbours.shape[0]
    element_count = element_nodes.shape[1]
    parted = wavefields.reshape(events, 2, 2, 3 * rows, WIDE)
    present = parted[:, :, 0].reshape(12 * rows, WIDE)
    earlier = parted[:, :, 1].reshape(12 * rows, WIDE)
    mass = inverse_mass.reshape(rows, WIDE)
    ids = jnp.pad(element_nodes, ((0, 3), (0, 0)), constant_values=NOWHERE)
    own = lax.axis_index("dom")
    peers = lax.dynamic_slice_in_dim(neighbours, own, 1, 0)
    slot_count, capacity = shared_points.shape[1:]
    live = jnp.arange(capacity, dtype=jnp.int32)[None, :] < shared_counts[0][:, None]
    slots = jnp.where(live, shared_points[0], NOWHERE)
    slots = jnp.pad(slots, ((0, 0), (0, WIDE - capacity)), constant_values=NOWHERE)
    slots = slots.reshape(12, 128)
    moduli = jnp.pad(moduli, ((0, 0), (0, 3), (0, 0)))
    det = jacobian_det.reshape(1, element_count)
    forward, backward, volume = (jnp.asarray(table) for table in padded_tables())
    common = (ids, inverse_jacobian, det, moduli, slots, peers, forward, backward, volume)
    vmem = pl.BlockSpec(memory_space=pltpu.VMEM)
    smem = pl.BlockSpec(memory_space=pltpu.SMEM)
    common_specs = [vmem, vmem, vmem, vmem, vmem, smem, vmem, vmem, vmem]
    state = jax.ShapeDtypeStruct((12 * rows, WIDE), f32)
    made = (
        state,
        jax.ShapeDtypeStruct((domains, 16, WIDE), f32),
        jax.ShapeDtypeStruct((2, 128, 128), f32),
    )
    scratch = [
        pltpu.VMEM((128, 12 * 128), f32),
        pltpu.VMEM((3 * 128, 12 * 128), f32),
        pltpu.VMEM((3 * 128, 12 * 128), f32),
        pltpu.VMEM((128, 12 * 128), f32),
        pltpu.VMEM((24 * rows, WIDE), f32),
    ]
    params = pltpu.CompilerParams(vmem_limit_bytes=50 * 1024 * 1024)

    def exchange(sending):
        return pl.pallas_call(
            swap_blocks,
            out_shape=jax.ShapeDtypeStruct(sending.shape, sending.dtype),
            in_specs=[vmem],
            out_specs=vmem,
            scratch_shapes=[
                pltpu.SemaphoreType.DMA((domains,)),
                pltpu.SemaphoreType.DMA((domains,)),
            ],
            compiler_params=pltpu.CompilerParams(collective_id=0, has_side_effects=True),
        )(sending)

    force, sending, terms = pl.pallas_call(
        first_step,
        out_shape=made,
        in_specs=[vmem] + common_specs,
        out_specs=(vmem,) * 3,
        scratch_shapes=scratch,
        compiler_params=params,
    )(present, *common)
    for _ in range(STEPS - 1):
        arrived = exchange(sending)
        following, force, sending, terms = pl.pallas_call(
            next_step,
            out_shape=(state,) + made,
            in_specs=[vmem] * 6 + common_specs,
            out_specs=(vmem,) * 4,
            scratch_shapes=scratch,
            compiler_params=params,
        )(present, earlier, force, arrived, mass, terms, *common)
        earlier, present = present, following
    arrived = exchange(sending)
    following = pl.pallas_call(
        combine,
        out_shape=state,
        in_specs=[vmem] * 6 + [smem],
        out_specs=vmem,
        compiler_params=params,
    )(present, earlier, force, arrived, mass, slots, peers)
    earlier, present = present, following

    sharers = lax.axis_size("event")
    share_width = element_count // sharers
    spot = lax.axis_index("event")
    terms = terms[:, :125]
    if sharers == 2:
        low, high = terms[:, :, :share_width], terms[:, :, share_width:]
        theirs = lax.ppermute(jnp.where(spot == 0, high, low), "event", [(0, 1), (1, 0)])
        summed = jnp.where(spot == 0, low, high) + theirs
    else:
        summed = lax.dynamic_slice_in_dim(
            lax.psum(terms, "event"), spot * share_width, share_width, 2
        )
    sensitivity = kernel_weight * time_step * summed
    next_wavefields = jnp.stack(
        [present.reshape(events, 2, 3, point_count), earlier.reshape(events, 2, 3, point_count)],
        axis=2,
    ).reshape(events, 12, point_count)
    return (next_wavefields, sensitivity)


def solution(mesh):
    return jax.shard_map(
        per_device,
        mesh=mesh,
        in_specs=(
            P(("groups", "event"), None, "dom"),
            P(None, "dom"),
            P(None, "dom"),
            P("dom"),
            P(None, None, "dom"),
            P("dom"),
            P(),
            P("dom", None),
            P("dom", None, None),
        ),
        out_specs=(P(("groups", "event"), None, "dom"), P("groups", None, ("dom", "event"))),
        check_vma=False,
    )
```

```python
import jax
import jax.numpy as jnp
import numpy as np
from jax import lax
from jax.experimental import pallas as pl
from jax.experimental.pallas import tpu as pltpu
from jax.sharding import PartitionSpec as P

STEPS = 2
WIDE = 256
NOWHERE = 1 << 24

time_step = 0.5
kernel_weight = 0.01
highest = lax.Precision.HIGHEST
f32 = jnp.float32
bf16 = jnp.bfloat16


def node_tables():
    points = np.array([-1.0, -np.sqrt(3.0 / 7.0), 0.0, np.sqrt(3.0 / 7.0), 1.0])
    legendre = (35.0 * points**4 - 30.0 * points**2 + 3.0) / 8.0
    derivative = np.zeros((5, 5))
    for a in range(5):
        for b in range(5):
            if a != b:
                derivative[a, b] = legendre[a] / (legendre[b] * (points[a] - points[b]))
    derivative[0, 0] = -5.0
    derivative[4, 4] = 5.0
    weights = np.array([0.1, 49.0 / 90.0, 32.0 / 45.0, 49.0 / 90.0, 0.1])
    cube_weights = weights[:, None, None] * weights[None, :, None] * weights[None, None, :]
    return (derivative, cube_weights)


def padded_tables():
    derivative, cube = node_tables()
    eye = np.eye(5)
    along = (
        np.kron(eye, np.kron(eye, derivative)),
        np.kron(eye, np.kron(derivative, eye)),
        np.kron(derivative, np.kron(eye, eye)),
    )
    forward = np.zeros((3 * 128, 128), np.float32)
    backward = np.zeros((128, 3 * 128), np.float32)
    for d in range(3):
        forward[d * 128 : d * 128 + 125, :125] = along[d]
        backward[:125, d * 128 : d * 128 + 125] = along[d].T
    volume = np.zeros((128, 128), np.float32)
    volume[:125] = cube.reshape(125, 1)
    return forward, backward, volume


def split(values):
    upper = values.astype(bf16)
    lower = (values - upper.astype(f32)).astype(bf16)
    return upper, lower


def columns_onehot(column_ids):
    return onehot_rows(column_ids, WIDE)


def onehot_rows(row_ids, count):
    rows = lax.broadcasted_iota(jnp.int32, (count, 128), 0).astype(f32).astype(bf16)
    wanted = jnp.broadcast_to(row_ids.astype(f32), (count, 128)).astype(bf16)
    return jnp.where(rows == wanted, jnp.ones((), bf16), jnp.zeros((), bf16))


def pick_rows(result, row_ids, group):
    mask = lax.broadcasted_iota(jnp.int32, (group, 128), 0) == row_ids
    return [
        jnp.sum(
            jnp.where(mask, result[c * group : (c + 1) * group], 0.0), axis=0, keepdims=True
        )
        for c in range(12)
    ]


def sum_sublanes(parts, sublane):
    for width in (4, 2, 1):
        first = (sublane & width) == 0
        merged = []
        for r in range(width):
            near = jnp.where(first, parts[r], parts[r + width])
            far = jnp.where(first, parts[r + width], parts[r])
            if width == 4:
                far = pltpu.roll(far, 4, 0)
            else:
                far = jnp.where(first, pltpu.roll(far, 8 - width, 0), pltpu.roll(far, width, 0))
            merged.append(near + far)
        parts = merged
    return parts[0]


def split_product(left, right):
    left_upper, left_lower = split(left)
    right_upper, right_lower = split(right)
    return jnp.dot(
        jnp.concatenate([left_upper, left_lower, left_upper], axis=1),
        jnp.concatenate([right_upper, right_upper, right_lower], axis=0),
        preferred_element_type=f32,
    )


def slot_onehot(slots_ref):
    return jnp.concatenate(
        [columns_onehot(slots_ref[r : r + 1, :] & (WIDE - 1)) for r in range(12)], axis=1
    )


def combine(present_ref, earlier_ref, force_ref, arrived_ref, mass_ref, slots_ref, peers_ref, following_ref):
    domains = arrived_ref.shape[0]
    rows = mass_ref.shape[0]
    blocks = []
    for k in range(6):
        block = jnp.zeros((16, WIDE), f32)
        for p in range(domains):
            block = jnp.where(peers_ref[0, k] == p, arrived_ref[p], block)
        blocks.append(block)
    received = jnp.concatenate(blocks, axis=1)
    onehot = slot_onehot(slots_ref)
    pieces = []
    for r in range(12):
        mask = lax.broadcasted_iota(jnp.int32, (8, 128), 0) == (slots_ref[r : r + 1, :] >> 8)
        part = received[:, r * 128 : (r + 1) * 128]
        pieces.append(
            jnp.concatenate(
                [jnp.where(mask, part[c : c + 1, :], 0.0) for c in range(12)], axis=0
            )
        )
    spread = jnp.concatenate(pieces, axis=1)
    upper, lower = split(spread)
    both = lax.dot_general(
        jnp.concatenate([upper, lower], axis=0), onehot, (((1,), (1,)), ((), ())),
        preferred_element_type=f32,
    )
    added = both[:96] + both[96:]
    mass = mass_ref[...] * (time_step * time_step)
    for c in range(12):
        where = slice(c * rows, (c + 1) * rows)
        force = force_ref[where, :]
        total = jnp.concatenate([force[:8] + added[c * 8 : (c + 1) * 8], force[8:]], axis=0)
        following_ref[where, :] = 2.0 * present_ref[where, :] - earlier_ref[where, :] - mass * total


def add_rows(g, values_ref, ids_ref, sum_ref, rows):
    base = pl.multiple_of(g * 8, 8)
    ids = ids_ref[pl.ds(base, 8), :]
    row_ids = ids >> 8
    column_ids = ids & (WIDE - 1)
    values = values_ref[pl.ds(base, 8), :]
    high = values.astype(bf16).astype(f32)
    low = values - high
    pieces = []
    columns = []
    for r in range(8):
        columns.append(columns_onehot(column_ids[r : r + 1, :]))
        chosen = onehot_rows(row_ids[r : r + 1, :], rows)
        blocks = []
        for part in (high, low):
            for c in range(12):
                row = jnp.broadcast_to(part[r : r + 1, c * 128 : (c + 1) * 128], (16, 128))
                row = row.astype(bf16)
                blocks += [chosen[t : t + 16] * row for t in range(0, rows, 16)]
        pieces.append(jnp.concatenate(blocks, axis=0))
    sum_ref[...] += lax.dot_general(
        jnp.concatenate(pieces, axis=1), jnp.concatenate(columns, axis=1),
        (((1,), (1,)), ((), ())), preferred_element_type=f32,
    )


def forces(
    present_ref, ids_ref, border_ids_ref, jacobian_ref, det_ref, moduli_ref, slots_ref, peers_ref,
    forward_ref, backward_ref, volume_ref,
    nodal_force_ref, sending_ref, terms_ref,
    nodal_ref, along_ref, traction_ref, packed_ref, sum_ref,
):
    rows = present_ref.shape[0] // 12
    sublane = lax.broadcasted_iota(jnp.int32, (8, 128), 0)
    tiles = rows // 8
    upper, lower = split(present_ref[...])
    table = jnp.concatenate([upper, lower], axis=1)

    def gather(g, carry):
        base = pl.multiple_of(g * 8, 8)
        ids = ids_ref[pl.ds(base, 8), :]
        onehot = jnp.concatenate(
            [columns_onehot((ids & (WIDE - 1))[r : r + 1, :]) for r in range(8)], axis=1
        )
        result = jnp.dot(
            table, jnp.concatenate([onehot, onehot], axis=0), preferred_element_type=f32
        )
        row_ids = ids >> 8
        masks = []
        for r in range(8):
            key = jnp.broadcast_to(row_ids[r : r + 1, :], (8, 128)) - sublane
            masks.append([key == 8 * t for t in range(tiles)])
        for c in range(12):
            found = [jnp.zeros((8, 128), f32)] * 8
            for r in range(8):
                for t in range(tiles):
                    first = c * rows + t * 8
                    tile = result[first : first + 8, r * 128 : (r + 1) * 128]
                    found[r] = jnp.where(masks[r][t], tile, found[r])
            nodal_ref[pl.ds(base, 8), c * 128 : (c + 1) * 128] = sum_sublanes(found, sublane)
        return carry

    lax.fori_loop(0, 16, gather, 0)
    along_ref[...] = split_product(forward_ref[...], nodal_ref[...])

    def elements(g, carry):
        base = pl.multiple_of(g * 8, 8)
        jac = [jnp.broadcast_to(jacobian_ref[i : i + 1, :], (8, 128)) for i in range(9)]
        shear = moduli_ref[0, pl.ds(base, 8), :]
        bulk = moduli_ref[1, pl.ds(base, 8), :]
        lame = bulk - 2.0 / 3.0 * shear
        volume = volume_ref[pl.ds(base, 8), :] * det_ref[...]
        scaled = [volume * jac[i] for i in range(9)]
        shear_sum = jnp.zeros((8, 128), f32)
        bulk_sum = jnp.zeros((8, 128), f32)
        for event in range(2):
            kept = []
            for field in range(2):
                first = (event * 2 + field) * 3
                local = [
                    [
                        along_ref[pl.ds(d * 128 + base, 8), (first + c) * 128 : (first + c + 1) * 128]
                        for c in range(3)
                    ]
                    for d in range(3)
                ]
                grad = [
                    [
                        local[0][c] * jac[m] + local[1][c] * jac[3 + m] + local[2][c] * jac[6 + m]
                        for c in range(3)
                    ]
                    for m in range(3)
                ]
                div = grad[0][0] + grad[1][1] + grad[2][2]
                strain = {}
                stress = {}
                deviator = {}
                for c in range(3):
                    for m in range(c, 3):
                        if c == m:
                            strain[c, m] = grad[c][c]
                            deviator[c, m] = strain[c, m] - div * (1.0 / 3.0)
                            stress[c, m] = 2.0 * shear * strain[c, m] + lame * div
                        else:
                            twice = grad[m][c] + grad[c][m]
                            strain[c, m] = 0.5 * twice
                            deviator[c, m] = strain[c, m]
                            stress[c, m] = shear * twice
                            stress[m, c] = stress[c, m]
                kept.append((deviator, div))
                for c in range(3):
                    for d in range(3):
                        traction_ref[
                            pl.ds(d * 128 + base, 8), (first + c) * 128 : (first + c + 1) * 128
                        ] = (
                            stress[c, 0] * scaled[3 * d]
                            + stress[c, 1] * scaled[3 * d + 1]
                            + stress[c, 2] * scaled[3 * d + 2]
                        )
            (dev0, div0), (dev1, div1) = kept
            bulk_sum = bulk_sum + div0 * div1
            for c in range(3):
                for m in range(c, 3):
                    product = dev0[c, m] * dev1[c, m]
                    shear_sum = shear_sum + (product if c == m else 2.0 * product)
        terms_ref[0, pl.ds(base, 8), :] += 2.0 * shear * shear_sum
        terms_ref[1, pl.ds(base, 8), :] += bulk * bulk_sum
        return carry

    lax.fori_loop(0, 16, elements, 0)
    nodal_force_ref[...] = split_product(backward_ref[...], traction_ref[...])
    lane = lax.broadcasted_iota(jnp.int32, (32, 128), 1)
    for c in range(12):
        column = slice(c * 128, (c + 1) * 128)
        packed = nodal_force_ref[:32, column]
        for b in range(1, 4):
            moved = pltpu.roll(nodal_force_ref[b * 32 : (b + 1) * 32, column], 32 * b, 1)
            packed = jnp.where(lane >= 32 * b, moved, packed)
        packed_ref[:, column] = packed
    sum_ref[...] = jnp.zeros_like(sum_ref)

    def border_rows(g, carry):
        add_rows(g, packed_ref, border_ids_ref, sum_ref, 16)
        return carry

    lax.fori_loop(0, 4, border_rows, 0)
    sums = sum_ref[:192, :] + sum_ref[192:, :]
    border = jnp.concatenate([sums[c * 16 : c * 16 + 8, :] for c in range(12)], axis=0)
    upper, lower = split(border)
    onehot = slot_onehot(slots_ref)
    result = jnp.dot(
        jnp.concatenate([upper, lower], axis=1),
        jnp.concatenate([onehot, onehot], axis=0),
        preferred_element_type=f32,
    )
    outgoing = []
    for r in range(12):
        picked = pick_rows(result[:, r * 128 : (r + 1) * 128], slots_ref[r : r + 1, :] >> 8, 8)
        outgoing.append(jnp.concatenate(picked + [jnp.zeros((4, 128), f32)], axis=0))
    for p in range(sending_ref.shape[0]):
        block = jnp.zeros((16, WIDE), f32)
        for k in range(6):
            block = jnp.where(
                peers_ref[0, k] == p,
                jnp.concatenate([outgoing[2 * k], outgoing[2 * k + 1]], axis=1),
                block,
            )
        sending_ref[p] = block


def swap_and_sum(
    sending_ref, nodal_force_ref, ids_ref, force_ref, arrived_ref, sum_ref, send_sem, recv_sem
):
    domains = sending_ref.shape[0]
    me = lax.axis_index("dom")
    barrier = pltpu.get_barrier_semaphore()
    for offset in range(1, domains):
        pl.semaphore_signal(
            barrier, inc=1, device_id={"dom": lax.rem(me + offset, domains)},
            device_id_type=pl.DeviceIdType.MESH,
        )
    pl.semaphore_wait(barrier, domains - 1)
    copies = []
    for offset in range(1, domains):
        target = lax.rem(me + offset, domains)
        copies.append(
            pltpu.make_async_remote_copy(
                src_ref=sending_ref.at[target],
                dst_ref=arrived_ref.at[me],
                send_sem=send_sem.at[offset],
                recv_sem=recv_sem.at[offset],
                device_id={"dom": target},
                device_id_type=pl.DeviceIdType.MESH,
            )
        )
        copies[-1].start()
    arrived_ref[me] = sending_ref[me]
    sum_ref[...] = jnp.zeros_like(sum_ref)
    half = sum_ref.shape[0] // 2

    def node_rows(g, carry):
        add_rows(g, nodal_force_ref, ids_ref, sum_ref, half // 12)
        return carry

    lax.fori_loop(0, 16, node_rows, 0)
    force_ref[...] = sum_ref[:half, :] + sum_ref[half:, :]
    for copy in copies:
        copy.wait()


def first_step(present_ref, *refs):
    refs[12][...] = jnp.zeros_like(refs[12])
    forces(present_ref, *refs)


def next_step(
    present_ref, earlier_ref, old_force_ref, arrived_ref, mass_ref, old_terms_ref,
    ids_ref, border_ids_ref, jacobian_ref, det_ref, moduli_ref, slots_ref, peers_ref,
    forward_ref, backward_ref, volume_ref,
    following_ref, nodal_force_ref, sending_ref, terms_ref, *scratch
):
    combine(present_ref, earlier_ref, old_force_ref, arrived_ref, mass_ref, slots_ref, peers_ref, following_ref)
    terms_ref[...] = old_terms_ref[...]
    forces(
        following_ref, ids_ref, border_ids_ref, jacobian_ref, det_ref, moduli_ref, slots_ref, peers_ref,
        forward_ref, backward_ref, volume_ref, nodal_force_ref, sending_ref, terms_ref, *scratch
    )


def per_device(
    wavefields,
    element_nodes,
    inverse_jacobian,
    jacobian_det,
    moduli,
    inverse_mass,
    neighbours,
    shared_counts,
    shared_points,
):
    events, _, point_count = wavefields.shape
    rows = point_count // WIDE
    domains = neighbours.shape[0]
    element_count = element_nodes.shape[1]
    parted = wavefields.reshape(events, 2, 2, 3 * rows, WIDE)
    present = parted[:, :, 0].reshape(12 * rows, WIDE)
    earlier = parted[:, :, 1].reshape(12 * rows, WIDE)
    mass = inverse_mass.reshape(rows, WIDE)
    ids = jnp.pad(element_nodes, ((0, 3), (0, 0)), constant_values=NOWHERE)
    own = lax.axis_index("dom")
    peers = lax.dynamic_slice_in_dim(neighbours, own, 1, 0)
    slot_count, capacity = shared_points.shape[1:]
    live = jnp.arange(capacity, dtype=jnp.int32)[None, :] < shared_counts[0][:, None]
    slots = jnp.where(live, shared_points[0], NOWHERE)
    slots = jnp.pad(slots, ((0, 0), (0, WIDE - capacity)), constant_values=NOWHERE)
    slots = slots.reshape(12, 128)
    moduli = jnp.pad(moduli, ((0, 0), (0, 3), (0, 0)))
    det = jacobian_det.reshape(1, element_count)
    forward, backward, volume = (jnp.asarray(table) for table in padded_tables())
    border_ids = jnp.concatenate([ids[b * 32 : (b + 1) * 32, :32] for b in range(4)], axis=1)
    common = (ids, border_ids, inverse_jacobian, det, moduli, slots, peers, forward, backward, volume)
    vmem = pl.BlockSpec(memory_space=pltpu.VMEM)
    smem = pl.BlockSpec(memory_space=pltpu.SMEM)
    common_specs = [vmem, vmem, vmem, vmem, vmem, vmem, smem, vmem, vmem, vmem]
    state = jax.ShapeDtypeStruct((12 * rows, WIDE), f32)
    made = (
        jax.ShapeDtypeStruct((128, 12 * 128), f32),
        jax.ShapeDtypeStruct((domains, 16, WIDE), f32),
        jax.ShapeDtypeStruct((2, 128, 128), f32),
    )
    scratch = [
        pltpu.VMEM((128, 12 * 128), f32),
        pltpu.VMEM((3 * 128, 12 * 128), f32),
        pltpu.VMEM((3 * 128, 12 * 128), f32),
        pltpu.VMEM((32, 12 * 128), f32),
        pltpu.VMEM((24 * 16, WIDE), f32),
    ]
    params = pltpu.CompilerParams(vmem_limit_bytes=50 * 1024 * 1024)

    def exchange(sending, nodal_force):
        return pl.pallas_call(
            swap_and_sum,
            out_shape=(state, jax.ShapeDtypeStruct(sending.shape, sending.dtype)),
            in_specs=[vmem] * 3,
            out_specs=(vmem, vmem),
            scratch_shapes=[
                pltpu.VMEM((24 * rows, WIDE), f32),
                pltpu.SemaphoreType.DMA((domains,)),
                pltpu.SemaphoreType.DMA((domains,)),
            ],
            compiler_params=pltpu.CompilerParams(
                collective_id=0, has_side_effects=True, vmem_limit_bytes=50 * 1024 * 1024
            ),
        )(sending, nodal_force, ids)

    nodal_force, sending, terms = pl.pallas_call(
        first_step,
        out_shape=made,
        in_specs=[vmem] + common_specs,
        out_specs=(vmem,) * 3,
        scratch_shapes=scratch,
        compiler_params=params,
    )(present, *common)
    for _ in range(STEPS - 1):
        force, arrived = exchange(sending, nodal_force)
        following, nodal_force, sending, terms = pl.pallas_call(
            next_step,
            out_shape=(state,) + made,
            in_specs=[vmem] * 6 + common_specs,
            out_specs=(vmem,) * 4,
            scratch_shapes=scratch,
            compiler_params=params,
        )(present, earlier, force, arrived, mass, terms, *common)
        earlier, present = present, following
    force, arrived = exchange(sending, nodal_force)
    following = pl.pallas_call(
        combine,
        out_shape=state,
        in_specs=[vmem] * 6 + [smem],
        out_specs=vmem,
        compiler_params=params,
    )(present, earlier, force, arrived, mass, slots, peers)
    earlier, present = present, following

    sharers = lax.axis_size("event")
    share_width = element_count // sharers
    spot = lax.axis_index("event")
    terms = terms[:, :125]
    if sharers == 2:
        low, high = terms[:, :, :share_width], terms[:, :, share_width:]
        theirs = lax.ppermute(jnp.where(spot == 0, high, low), "event", [(0, 1), (1, 0)])
        summed = jnp.where(spot == 0, low, high) + theirs
    else:
        summed = lax.dynamic_slice_in_dim(
            lax.psum(terms, "event"), spot * share_width, share_width, 2
        )
    sensitivity = kernel_weight * time_step * summed
    next_wavefields = jnp.stack(
        [present.reshape(events, 2, 3, point_count), earlier.reshape(events, 2, 3, point_count)],
        axis=2,
    ).reshape(events, 12, point_count)
    return (next_wavefields, sensitivity)


def solution(mesh):
    return jax.shard_map(
        per_device,
        mesh=mesh,
        in_specs=(
            P(("groups", "event"), None, "dom"),
            P(None, "dom"),
            P(None, "dom"),
            P("dom"),
            P(None, None, "dom"),
            P("dom"),
            P(),
            P("dom", None),
            P("dom", None, None),
        ),
        out_specs=(P(("groups", "event"), None, "dom"), P("groups", None, ("dom", "event"))),
        check_vma=False,
    )
```

```python
import jax
import jax.numpy as jnp
import numpy as np
from jax import lax
from jax.experimental import pallas as pl
from jax.experimental.pallas import tpu as pltpu
from jax.sharding import PartitionSpec as P

STEPS = 2
WIDE = 256
NOWHERE = 1 << 24

time_step = 0.5
kernel_weight = 0.01
highest = lax.Precision.HIGHEST
f32 = jnp.float32
bf16 = jnp.bfloat16


def node_tables():
    points = np.array([-1.0, -np.sqrt(3.0 / 7.0), 0.0, np.sqrt(3.0 / 7.0), 1.0])
    legendre = (35.0 * points**4 - 30.0 * points**2 + 3.0) / 8.0
    derivative = np.zeros((5, 5))
    for a in range(5):
        for b in range(5):
            if a != b:
                derivative[a, b] = legendre[a] / (legendre[b] * (points[a] - points[b]))
    derivative[0, 0] = -5.0
    derivative[4, 4] = 5.0
    weights = np.array([0.1, 49.0 / 90.0, 32.0 / 45.0, 49.0 / 90.0, 0.1])
    cube_weights = weights[:, None, None] * weights[None, :, None] * weights[None, None, :]
    return (derivative, cube_weights)


def padded_tables():
    derivative, cube = node_tables()
    eye = np.eye(5)
    along = (
        np.kron(eye, np.kron(eye, derivative)),
        np.kron(eye, np.kron(derivative, eye)),
        np.kron(derivative, np.kron(eye, eye)),
    )
    forward = np.zeros((3 * 128, 128), np.float32)
    backward = np.zeros((128, 3 * 128), np.float32)
    for d in range(3):
        forward[d * 128 : d * 128 + 125, :125] = along[d]
        backward[:125, d * 128 : d * 128 + 125] = along[d].T
    volume = np.zeros((128, 128), np.float32)
    volume[:125] = cube.reshape(125, 1)
    return forward, backward, volume


def split(values):
    upper = values.astype(bf16)
    lower = (values - upper.astype(f32)).astype(bf16)
    return upper, lower


def columns_onehot(column_ids):
    return onehot_rows(column_ids, WIDE)


def onehot_rows(row_ids, count):
    rows = lax.broadcasted_iota(jnp.int32, (count, 128), 0).astype(f32).astype(bf16)
    wanted = jnp.broadcast_to(row_ids.astype(f32), (count, 128)).astype(bf16)
    return jnp.where(rows == wanted, jnp.ones((), bf16), jnp.zeros((), bf16))


def pick_rows(result, row_ids, group):
    mask = lax.broadcasted_iota(jnp.int32, (group, 128), 0) == row_ids
    return [
        jnp.sum(
            jnp.where(mask, result[c * group : (c + 1) * group], 0.0), axis=0, keepdims=True
        )
        for c in range(12)
    ]


def sum_sublanes(parts, sublane):
    for width in (4, 2, 1):
        first = (sublane & width) == 0
        merged = []
        for r in range(width):
            near = jnp.where(first, parts[r], parts[r + width])
            far = jnp.where(first, parts[r + width], parts[r])
            if width == 4:
                far = pltpu.roll(far, 4, 0)
            else:
                far = jnp.where(first, pltpu.roll(far, 8 - width, 0), pltpu.roll(far, width, 0))
            merged.append(near + far)
        parts = merged
    return parts[0]


def split_product(left, right):
    left_upper, left_lower = split(left)
    right_upper, right_lower = split(right)
    return jnp.dot(
        jnp.concatenate([left_upper, left_lower, left_upper], axis=1),
        jnp.concatenate([right_upper, right_upper, right_lower], axis=0),
        preferred_element_type=f32,
    )


def slot_onehot(slots_ref):
    return jnp.concatenate(
        [columns_onehot(slots_ref[r : r + 1, :] & (WIDE - 1)) for r in range(12)], axis=1
    )


def combine(present_ref, earlier_ref, force_ref, arrived_ref, mass_ref, slots_ref, peers_ref, following_ref):
    domains = arrived_ref.shape[0]
    rows = mass_ref.shape[0]
    blocks = []
    for k in range(6):
        block = jnp.zeros((16, WIDE), f32)
        for p in range(domains):
            block = jnp.where(peers_ref[0, k] == p, arrived_ref[p], block)
        blocks.append(block)
    received = jnp.concatenate(blocks, axis=1)
    onehot = slot_onehot(slots_ref)
    pieces = []
    for r in range(12):
        mask = lax.broadcasted_iota(jnp.int32, (8, 128), 0) == (slots_ref[r : r + 1, :] >> 8)
        part = received[:, r * 128 : (r + 1) * 128]
        pieces.append(
            jnp.concatenate(
                [jnp.where(mask, part[c : c + 1, :], 0.0) for c in range(12)], axis=0
            )
        )
    spread = jnp.concatenate(pieces, axis=1)
    upper, lower = split(spread)
    both = lax.dot_general(
        jnp.concatenate([upper, lower], axis=0), onehot, (((1,), (1,)), ((), ())),
        preferred_element_type=f32,
    )
    added = both[:96] + both[96:]
    mass = mass_ref[...] * (time_step * time_step)
    for c in range(12):
        where = slice(c * rows, (c + 1) * rows)
        force = force_ref[where, :]
        total = jnp.concatenate([force[:8] + added[c * 8 : (c + 1) * 8], force[8:]], axis=0)
        following_ref[where, :] = 2.0 * present_ref[where, :] - earlier_ref[where, :] - mass * total


def add_rows(g, values_ref, ids_ref, sum_ref, rows):
    base = pl.multiple_of(g * 8, 8)
    ids = ids_ref[pl.ds(base, 8), :]
    row_ids = ids >> 8
    column_ids = ids & (WIDE - 1)
    values = values_ref[pl.ds(base, 8), :]
    high = values.astype(bf16).astype(f32)
    low = values - high
    pieces = []
    columns = []
    for r in range(8):
        columns.append(columns_onehot(column_ids[r : r + 1, :]))
        chosen = onehot_rows(row_ids[r : r + 1, :], rows)
        blocks = []
        for part in (high, low):
            for c in range(12):
                row = jnp.broadcast_to(part[r : r + 1, c * 128 : (c + 1) * 128], (16, 128))
                row = row.astype(bf16)
                blocks += [chosen[t : t + 16] * row for t in range(0, rows, 16)]
        pieces.append(jnp.concatenate(blocks, axis=0))
    sum_ref[...] += lax.dot_general(
        jnp.concatenate(pieces, axis=1), jnp.concatenate(columns, axis=1),
        (((1,), (1,)), ((), ())), preferred_element_type=f32,
    )


def forces(
    present_ref, ids_ref, border_ids_ref, jacobian_ref, det_ref, moduli_ref, slots_ref, peers_ref,
    forward_ref, backward_ref, volume_ref,
    nodal_force_ref, sending_ref, terms_ref,
    nodal_ref, along_ref, traction_ref, packed_ref, sum_ref,
):
    rows = present_ref.shape[0] // 12
    sublane = lax.broadcasted_iota(jnp.int32, (8, 128), 0)
    tiles = rows // 8
    upper, lower = split(present_ref[...])
    table = jnp.concatenate([upper, lower], axis=1)

    def gather(g, carry):
        base = pl.multiple_of(g * 8, 8)
        ids = ids_ref[pl.ds(base, 8), :]
        onehot = jnp.concatenate(
            [columns_onehot((ids & (WIDE - 1))[r : r + 1, :]) for r in range(8)], axis=1
        )
        result = jnp.dot(
            table, jnp.concatenate([onehot, onehot], axis=0), preferred_element_type=f32
        )
        row_ids = ids >> 8
        masks = []
        for r in range(8):
            key = jnp.broadcast_to(row_ids[r : r + 1, :], (8, 128)) - sublane
            masks.append([key == 8 * t for t in range(tiles)])
        for c in range(12):
            found = [jnp.zeros((8, 128), f32)] * 8
            for r in range(8):
                for t in range(tiles):
                    first = c * rows + t * 8
                    tile = result[first : first + 8, r * 128 : (r + 1) * 128]
                    found[r] = jnp.where(masks[r][t], tile, found[r])
            nodal_ref[pl.ds(base, 8), c * 128 : (c + 1) * 128] = sum_sublanes(found, sublane)
        return carry

    lax.fori_loop(0, 16, gather, 0)
    along_ref[...] = split_product(forward_ref[...], nodal_ref[...])

    def elements(g, carry):
        base = pl.multiple_of(g * 8, 8)
        jac = [jnp.broadcast_to(jacobian_ref[i : i + 1, :], (8, 128)) for i in range(9)]
        shear = moduli_ref[0, pl.ds(base, 8), :]
        bulk = moduli_ref[1, pl.ds(base, 8), :]
        lame = bulk - 2.0 / 3.0 * shear
        volume = volume_ref[pl.ds(base, 8), :] * det_ref[...]
        scaled = [volume * jac[i] for i in range(9)]
        shear_sum = jnp.zeros((8, 128), f32)
        bulk_sum = jnp.zeros((8, 128), f32)
        for event in range(2):
            kept = []
            for field in range(2):
                first = (event * 2 + field) * 3
                local = [
                    [
                        along_ref[pl.ds(d * 128 + base, 8), (first + c) * 128 : (first + c + 1) * 128]
                        for c in range(3)
                    ]
                    for d in range(3)
                ]
                grad = [
                    [
                        local[0][c] * jac[m] + local[1][c] * jac[3 + m] + local[2][c] * jac[6 + m]
                        for c in range(3)
                    ]
                    for m in range(3)
                ]
                div = grad[0][0] + grad[1][1] + grad[2][2]
                strain = {}
                stress = {}
                deviator = {}
                for c in range(3):
                    for m in range(c, 3):
                        if c == m:
                            strain[c, m] = grad[c][c]
                            deviator[c, m] = strain[c, m] - div * (1.0 / 3.0)
                            stress[c, m] = 2.0 * shear * strain[c, m] + lame * div
                        else:
                            twice = grad[m][c] + grad[c][m]
                            strain[c, m] = 0.5 * twice
                            deviator[c, m] = strain[c, m]
                            stress[c, m] = shear * twice
                            stress[m, c] = stress[c, m]
                kept.append((deviator, div))
                for c in range(3):
                    for d in range(3):
                        traction_ref[
                            pl.ds(d * 128 + base, 8), (first + c) * 128 : (first + c + 1) * 128
                        ] = (
                            stress[c, 0] * scaled[3 * d]
                            + stress[c, 1] * scaled[3 * d + 1]
                            + stress[c, 2] * scaled[3 * d + 2]
                        )
            (dev0, div0), (dev1, div1) = kept
            bulk_sum = bulk_sum + div0 * div1
            for c in range(3):
                for m in range(c, 3):
                    product = dev0[c, m] * dev1[c, m]
                    shear_sum = shear_sum + (product if c == m else 2.0 * product)
        terms_ref[0, pl.ds(base, 8), :] += 2.0 * shear * shear_sum
        terms_ref[1, pl.ds(base, 8), :] += bulk * bulk_sum
        return carry

    lax.fori_loop(0, 16, elements, 0)
    nodal_force_ref[...] = split_product(backward_ref[...], traction_ref[...])
    lane = lax.broadcasted_iota(jnp.int32, (32, 128), 1)
    for c in range(12):
        column = slice(c * 128, (c + 1) * 128)
        packed = nodal_force_ref[:32, column]
        for b in range(1, 4):
            moved = pltpu.roll(nodal_force_ref[b * 32 : (b + 1) * 32, column], 32 * b, 1)
            packed = jnp.where(lane >= 32 * b, moved, packed)
        packed_ref[:, column] = packed
    sum_ref[...] = jnp.zeros_like(sum_ref)

    def border_rows(g, carry):
        add_rows(g, packed_ref, border_ids_ref, sum_ref, 16)
        return carry

    lax.fori_loop(0, 4, border_rows, 0)
    sums = sum_ref[:192, :] + sum_ref[192:, :]
    border = jnp.concatenate([sums[c * 16 : c * 16 + 8, :] for c in range(12)], axis=0)
    upper, lower = split(border)
    onehot = slot_onehot(slots_ref)
    result = jnp.dot(
        jnp.concatenate([upper, lower], axis=1),
        jnp.concatenate([onehot, onehot], axis=0),
        preferred_element_type=f32,
    )
    outgoing = []
    for r in range(12):
        picked = pick_rows(result[:, r * 128 : (r + 1) * 128], slots_ref[r : r + 1, :] >> 8, 8)
        outgoing.append(jnp.concatenate(picked + [jnp.zeros((4, 128), f32)], axis=0))
    for p in range(sending_ref.shape[0]):
        block = jnp.zeros((16, WIDE), f32)
        for k in range(6):
            block = jnp.where(
                peers_ref[0, k] == p,
                jnp.concatenate([outgoing[2 * k], outgoing[2 * k + 1]], axis=1),
                block,
            )
        sending_ref[p] = block


def step(
    present_ref, earlier_ref, mass_ref, old_terms_ref,
    ids_ref, border_ids_ref, jacobian_ref, det_ref, moduli_ref, slots_ref, peers_ref,
    forward_ref, backward_ref, volume_ref,
    following_ref, terms_ref, other_terms_ref,
    nodal_ref, along_ref, traction_ref, packed_ref, border_sum_ref,
    nodal_force_ref, sending_ref, arrived_ref, force_ref, sum_ref, send_sem, recv_sem,
):
    domains = sending_ref.shape[0]
    me = lax.axis_index("dom")
    barrier = pltpu.get_barrier_semaphore()
    for offset in range(1, domains):
        pl.semaphore_signal(
            barrier, inc=1, device_id={"dom": lax.rem(me + offset, domains)},
            device_id_type=pl.DeviceIdType.MESH,
        )
    sharer = {"event": 1 - lax.axis_index("event")}
    pl.semaphore_signal(
        barrier, inc=1, device_id=sharer, device_id_type=pl.DeviceIdType.MESH
    )
    terms_ref[...] = old_terms_ref[...]
    forces(
        present_ref, ids_ref, border_ids_ref, jacobian_ref, det_ref, moduli_ref, slots_ref,
        peers_ref, forward_ref, backward_ref, volume_ref,
        nodal_force_ref, sending_ref, terms_ref,
        nodal_ref, along_ref, traction_ref, packed_ref, border_sum_ref,
    )
    pl.semaphore_wait(barrier, domains)
    copies = []
    for offset in range(1, domains):
        target = lax.rem(me + offset, domains)
        copies.append(
            pltpu.make_async_remote_copy(
                src_ref=sending_ref.at[target],
                dst_ref=arrived_ref.at[me],
                send_sem=send_sem.at[offset],
                recv_sem=recv_sem.at[offset],
                device_id={"dom": target},
                device_id_type=pl.DeviceIdType.MESH,
            )
        )
        copies[-1].start()
    copies.append(
        pltpu.make_async_remote_copy(
            src_ref=terms_ref,
            dst_ref=other_terms_ref,
            send_sem=send_sem.at[0],
            recv_sem=recv_sem.at[0],
            device_id=sharer,
            device_id_type=pl.DeviceIdType.MESH,
        )
    )
    copies[-1].start()
    arrived_ref[me] = sending_ref[me]
    sum_ref[...] = jnp.zeros_like(sum_ref)
    half = sum_ref.shape[0] // 2

    def node_rows(g, carry):
        add_rows(g, nodal_force_ref, ids_ref, sum_ref, half // 12)
        return carry

    lax.fori_loop(0, 16, node_rows, 0)
    force_ref[...] = sum_ref[:half, :] + sum_ref[half:, :]
    for copy in copies:
        copy.wait()
    combine(
        present_ref, earlier_ref, force_ref, arrived_ref, mass_ref, slots_ref, peers_ref,
        following_ref,
    )


def per_device(
    wavefields,
    element_nodes,
    inverse_jacobian,
    jacobian_det,
    moduli,
    inverse_mass,
    neighbours,
    shared_counts,
    shared_points,
):
    events, _, point_count = wavefields.shape
    rows = point_count // WIDE
    domains = neighbours.shape[0]
    element_count = element_nodes.shape[1]
    parted = wavefields.reshape(events, 2, 2, 3 * rows, WIDE)
    present = parted[:, :, 0].reshape(12 * rows, WIDE)
    earlier = parted[:, :, 1].reshape(12 * rows, WIDE)
    mass = inverse_mass.reshape(rows, WIDE)
    ids = jnp.pad(element_nodes, ((0, 3), (0, 0)), constant_values=NOWHERE)
    own = lax.axis_index("dom")
    peers = lax.dynamic_slice_in_dim(neighbours, own, 1, 0)
    slot_count, capacity = shared_points.shape[1:]
    live = jnp.arange(capacity, dtype=jnp.int32)[None, :] < shared_counts[0][:, None]
    slots = jnp.where(live, shared_points[0], NOWHERE)
    slots = jnp.pad(slots, ((0, 0), (0, WIDE - capacity)), constant_values=NOWHERE)
    slots = slots.reshape(12, 128)
    moduli = jnp.pad(moduli, ((0, 0), (0, 3), (0, 0)))
    det = jacobian_det.reshape(1, element_count)
    forward, backward, volume = (jnp.asarray(table) for table in padded_tables())
    border_ids = jnp.concatenate([ids[b * 32 : (b + 1) * 32, :32] for b in range(4)], axis=1)
    common = (ids, border_ids, inverse_jacobian, det, moduli, slots, peers, forward, backward, volume)
    vmem = pl.BlockSpec(memory_space=pltpu.VMEM)
    smem = pl.BlockSpec(memory_space=pltpu.SMEM)
    common_specs = [vmem, vmem, vmem, vmem, vmem, vmem, smem, vmem, vmem, vmem]
    state = jax.ShapeDtypeStruct((12 * rows, WIDE), f32)
    blocks = (domains, 16, WIDE)
    terms = jnp.zeros((2, 128, 128), f32)
    take_step = pl.pallas_call(
        step,
        out_shape=(state,) + (jax.ShapeDtypeStruct(terms.shape, f32),) * 2,
        in_specs=[vmem] * 4 + common_specs,
        out_specs=(vmem,) * 3,
        scratch_shapes=[
            pltpu.VMEM((128, 12 * 128), f32),
            pltpu.VMEM((3 * 128, 12 * 128), f32),
            pltpu.VMEM((3 * 128, 12 * 128), f32),
            pltpu.VMEM((32, 12 * 128), f32),
            pltpu.VMEM((24 * 16, WIDE), f32),
            pltpu.VMEM((128, 12 * 128), f32),
            pltpu.VMEM(blocks, f32),
            pltpu.VMEM(blocks, f32),
            pltpu.VMEM((12 * rows, WIDE), f32),
            pltpu.VMEM((24 * rows, WIDE), f32),
            pltpu.SemaphoreType.DMA((domains,)),
            pltpu.SemaphoreType.DMA((domains,)),
        ],
        compiler_params=pltpu.CompilerParams(
            collective_id=0, has_side_effects=True, vmem_limit_bytes=50 * 1024 * 1024
        ),
    )
    for _ in range(STEPS):
        following, terms, other_terms = take_step(present, earlier, mass, terms, *common)
        earlier, present = present, following

    share_width = element_count // lax.axis_size("event")
    both = (terms + other_terms)[:, :125]
    summed = jnp.where(
        lax.axis_index("event") == 0, both[:, :, :share_width], both[:, :, share_width:]
    )
    sensitivity = kernel_weight * time_step * summed
    next_wavefields = jnp.stack(
        [present.reshape(events, 2, 3, point_count), earlier.reshape(events, 2, 3, point_count)],
        axis=2,
    ).reshape(events, 12, point_count)
    return (next_wavefields, sensitivity)


def solution(mesh):
    return jax.shard_map(
        per_device,
        mesh=mesh,
        in_specs=(
            P(("groups", "event"), None, "dom"),
            P(None, "dom"),
            P(None, "dom"),
            P("dom"),
            P(None, None, "dom"),
            P("dom"),
            P(),
            P("dom", None),
            P("dom", None, None),
        ),
        out_specs=(P(("groups", "event"), None, "dom"), P("groups", None, ("dom", "event"))),
        check_vma=False,
    )
```
